32 devices in a mesh: team: 4 (over x, core), env: 8 (over z, y).
Axes of the slice: x: 2, y: 2, z: 4, core: 2. Of those that a mesh axis runs over, the one named last changes fastest.
Arguments:
- features: bfloat16 [16384, 512], P(('team', 'env')), may hold values from -7 to 7
- team_of: int32 [16384], P(('team', 'env')), may hold values from 0 to 3, as said below
- env_of: int32 [16384], P(('team', 'env')), may hold values from 0 to 63, as said below
- actions: int32 [16384], P(('team', 'env')), may hold values from 0 to 127
- old_logp: float32 [16384], P(('team', 'env')), as said below
- advantages: float32 [16384], P(('team', 'env')), may hold values from -4 to 9
- returns: bfloat16 [16384], P(('team', 'env')), may hold values from -4 to 4
- w_hidden: bfloat16 [512, 512], replicated, may hold values from -0.25 to 0.25
- w_comm: bfloat16 [512, 512], replicated, may hold values from -0.25 to 0.25
- w_policy: bfloat16 [512, 128], replicated, may hold values from -0.25 to 0.25
- norm_gain: float32 [512], replicated, may hold values from 0.5 to 1.5
- w_query: bfloat16 [512, 512], replicated, may hold values from -0.25 to 0.25
- w_key: bfloat16 [512, 512], replicated, may hold values from -0.25 to 0.25
- w_value: float32 [512], replicated, may hold values from -0.25 to 0.25
Outputs:
- grad_input: bfloat16 [16384, 512], P(('team', 'env'))
- grad_w_hidden: float32 [512, 512], P(('team', 'env'))
- grad_w_comm: float32 [512, 512], P(('team', 'env'))
- grad_w_policy: float32 [512, 128], P(('team', 'env'))
- grad_w_query: float32 [512, 512], P(('team', 'env'))
- grad_w_key: float32 [512, 512], P(('team', 'env'))
The draws below stay inside these ranges and needn't reach their ends.
Inputs may be any that keep to these rules, and one draw needn't show every extreme that they name: `team_of`: rows form 4 * 8 blocks of 512, block b = t * 8 + e; over the blocks that share e, each team number names exactly 512 agents. `env_of`: block b = t * 8 + e of 512 rows holds exactly 32 agents of each environment (t * 8 + j) * 2 + l, 0 <= j < 8, 0 <= l < 2, and no others. `old_logp`: within 1.5 of -ln(128).
All inputs are finite; a program needn't handle non-finite values.
Results may differ from the reference program's by a relative error of at most 0.0077.
Values may be sent and summed in bfloat16 or wider, within the bound.
A program may use at most 64 MiB of HBM per device.

```python
import math
import jax
import jax.numpy as jnp
from jax import lax

D = 512
HEADS = 4
ACTIONS = 128
TEAMS = 4
ENV_AGENTS = 256
ENV_DEV = 2
ROWS = 512
TEAM_DEVS = 4
ENV_DEVS = 8
AGENTS = 16384
ENVS = 64
TEAM_SIZE = 512


def team_ids(key):
    base_key = jax.random.fold_in(key, 101)
    key_list = jax.random.split(base_key, ENV_DEVS)
    spread = jax.vmap(lambda single: jax.random.permutation(single, TEAM_DEVS * ROWS))(key_list) % TEAMS
    return jnp.transpose(spread.reshape(ENV_DEVS, TEAM_DEVS, ROWS), (1, 0, 2)).reshape(AGENTS).astype(jnp.int32)


def draw_team_of(key, part):
    return team_ids(key)


def draw_env_of(key, part):
    base_key = jax.random.fold_in(key, 202)
    key_list = jax.random.split(base_key, TEAM_DEVS * ENV_DEVS)
    slot_table = jax.vmap(lambda single: jax.random.permutation(single, ROWS))(key_list)
    block_index = jnp.arange(TEAM_DEVS * ENV_DEVS, dtype=jnp.int32)[:, None]
    line_index = block_index // ENV_DEVS
    target = slot_table % ENV_DEVS
    local_env = slot_table // ENV_DEVS % ENV_DEV
    return ((line_index * ENV_DEVS + target) * ENV_DEV + local_env).reshape(AGENTS).astype(jnp.int32)


def draw_features(key, part):
    team_number = team_ids(key)
    block_index = jnp.arange(AGENTS, dtype=jnp.int32) // ROWS
    group_index = block_index % ENV_DEVS
    line_index = block_index // ENV_DEVS
    rising = 1.0 + 2.0 * line_index.astype(jnp.float32) / max(TEAM_DEVS - 1, 1)
    centers = jax.random.truncated_normal(jax.random.fold_in(key, 303), -4.0, 4.0, (ENV_DEVS * TEAMS, D), jnp.float32)
    jitter = jax.random.truncated_normal(jax.random.fold_in(key, 304), -4.0, 4.0, (AGENTS, D), jnp.float32)
    picked = centers[group_index * TEAMS + team_number]
    return (0.7 * jitter + 0.35 * rising[:, None] * picked).astype(jnp.bfloat16)


def draw_advantages(key, part):
    block_index = jnp.arange(AGENTS, dtype=jnp.int32) // ROWS
    rising = 1.0 + 2.0 * block_index.astype(jnp.float32) / max(TEAM_DEVS * ENV_DEVS - 1, 1)
    jitter = jax.random.truncated_normal(jax.random.fold_in(key, 404), -4.0, 4.0, (AGENTS,), jnp.float32)
    return (jitter + rising).astype(jnp.float32)


def draw_old_logp(key, part):
    base_key = jax.random.fold_in(key, 505)
    jitter = jax.random.uniform(base_key, (AGENTS,), jnp.float32, -1.0, 1.0)
    return (jitter - math.log(ACTIONS)).astype(jnp.float32)


def plant(result, stream_key, smallest, largest):
    spot = [jax.random.randint(jax.random.fold_in(stream_key, axis), (), 0, length) for axis, length in enumerate(result.shape)]
    widest = result.shape.index(max(result.shape))
    neighbour = spot[:widest] + [(spot[widest] + 1) % result.shape[widest]] + spot[widest + 1:]
    return result.at[tuple(spot)].set(smallest).at[tuple(neighbour)].set(largest)


def level_of(stream_key, dims, cuts, low, top_value):
    factor_of = 1.0
    for axis_at, shards_of in cuts:
        steps = jax.random.uniform(jax.random.fold_in(jax.random.fold_in(stream_key, 6), axis_at), (shards_of,), jnp.float32, low / len(cuts), top_value / len(cuts))
        factor_of = factor_of * jnp.repeat(jnp.exp(steps), dims[axis_at] // shards_of).reshape((-1,) + (1,) * (len(dims) - 1 - axis_at))
    return factor_of


def gaussian(own_key, extent, deviation, limit, pieces=(), held_as=jnp.bfloat16):
    gain = level_of(own_key, extent, pieces, -0.22, 0.18) if pieces else 1.0
    array = jax.random.normal(own_key, extent, jnp.float32) * deviation * gain
    return jnp.minimum(jnp.maximum(array, -limit), limit).astype(held_as)


def setup_inputs(seed: int = 0) -> dict:
    seeds = jax.random.split(jax.random.key(seed), 15)
    return {
        "features": draw_features(jax.random.fold_in(seeds[14], 71), 0),
        "team_of": draw_team_of(jax.random.fold_in(seeds[14], 71), 0),
        "env_of": draw_env_of(jax.random.fold_in(seeds[14], 71), 0),
        "actions": plant(jax.random.randint(seeds[3], (AGENTS,), 0, ACTIONS), jax.random.fold_in(seeds[3], 1), 0, ACTIONS - 1).astype(jnp.int32),
        "old_logp": draw_old_logp(jax.random.fold_in(seeds[14], 71), 0),
        "advantages": draw_advantages(jax.random.fold_in(seeds[14], 71), 0),
        "returns": gaussian(seeds[6], (AGENTS,), 1.0, 4.0, ((0, 32),)),
        "w_hidden": gaussian(seeds[7], (D, D), D ** -0.5, 0.25),
        "w_comm": gaussian(seeds[8], (D, D), D ** -0.5, 0.25),
        "w_policy": gaussian(seeds[9], (D, ACTIONS), D ** -0.5, 0.25),
        "norm_gain": jnp.clip(1.0 + 0.1 * jax.random.normal(seeds[10], (D,), jnp.float32), 0.5, 1.5),
        "w_query": gaussian(seeds[11], (D, D), D ** -0.5, 0.25),
        "w_key": gaussian(seeds[12], (D, D), D ** -0.5, 0.25),
        "w_value": gaussian(seeds[13], (D,), D ** -0.5, 0.25, (), jnp.float32),
    }


KL_WEIGHT = 0.5
NORM_EPS = 1e-05

def lowered(values):
    return lax.optimization_barrier(values.astype(jnp.bfloat16))

def matmul(left_side, right_side):
    return jnp.dot(left_side.astype(jnp.float32), right_side.astype(jnp.float32), preferred_element_type=jnp.float32)

def normalize(values):
    center = values - lax.optimization_barrier(jnp.mean(values, axis=-1, keepdims=True))
    spread = jnp.sqrt(lax.optimization_barrier(jnp.mean(center * center, axis=-1, keepdims=True)) + NORM_EPS)
    return (center / spread, spread)

def normalize_back(gradient, normed, spread):
    mean_grad = lax.optimization_barrier(jnp.mean(gradient, axis=-1, keepdims=True))
    mean_along = lax.optimization_barrier(jnp.mean(gradient * normed, axis=-1, keepdims=True))
    return (gradient - mean_grad - normed * mean_along) / spread

def critic_env(inputs, targets, norm_gain, w_query, w_key, w_value):
    head_width = D // HEADS
    factor = 1.0 / math.sqrt(head_width)
    rows_in = inputs.astype(jnp.float32)
    input_hat, input_spread = normalize(rows_in)
    normed = lowered(input_hat * norm_gain)
    query_rows = lowered(matmul(normed, w_query))
    key_rows = lowered(matmul(normed, w_key))
    head_shape = (ENV_AGENTS, HEADS, head_width)
    query_heads = query_rows.reshape(head_shape).astype(jnp.float32)
    key_heads = key_rows.reshape(head_shape).astype(jnp.float32)
    value_heads = normed.reshape(head_shape).astype(jnp.float32)
    scores = jnp.einsum('qhd,khd->hqk', query_heads, key_heads) * factor
    raised = jnp.exp(scores)
    attention = raised / lax.optimization_barrier(jnp.sum(raised, axis=-1, keepdims=True))
    attention_low = lowered(attention).astype(jnp.float32)
    attended = jnp.einsum('hqk,khd->qhd', attention_low, value_heads)
    mixed = rows_in + attended.reshape(ENV_AGENTS, D)
    mixed_hat, mixed_spread = normalize(mixed)
    value_out = lax.optimization_barrier(jnp.sum(mixed_hat * w_value, axis=-1))
    value_grad = value_out - targets.astype(jnp.float32)
    mixed_grad = normalize_back(value_grad[:, None] * w_value, mixed_hat, mixed_spread)
    out_grad = lowered(mixed_grad).reshape(head_shape).astype(jnp.float32)
    prob_grad = jnp.einsum('qhd,khd->hqk', out_grad, value_heads)
    value_side = jnp.einsum('hqk,qhd->khd', attention_low, out_grad)
    score_grad = attention * (prob_grad - lax.optimization_barrier(jnp.sum(attention * prob_grad, axis=-1, keepdims=True))) * factor
    score_low = lowered(score_grad).astype(jnp.float32)
    query_grad = lowered(jnp.einsum('hqk,khd->qhd', score_low, key_heads)).reshape(ENV_AGENTS, D)
    key_grad = lowered(jnp.einsum('hqk,qhd->khd', score_low, query_heads)).reshape(ENV_AGENTS, D)
    normed_grad = matmul(query_grad, w_query.T) + matmul(key_grad, w_key.T) + value_side.reshape(ENV_AGENTS, D)
    input_grad = mixed_grad + normalize_back(normed_grad * norm_gain, input_hat, input_spread)
    return (lowered(input_grad), normed, query_grad, key_grad)

def reference(features, team_of, env_of, actions, old_logp, advantages, returns, w_hidden, w_comm, w_policy, norm_gain, w_query, w_key, w_value):
    inv_peers = 1.0 / (TEAM_SIZE - 1)
    block_of = jnp.arange(AGENTS, dtype=jnp.int32) // ROWS
    team_index = block_of % ENV_DEVS * TEAMS + team_of.astype(jnp.int32)
    feature_full = features.astype(jnp.float32)
    team_sums = jax.ops.segment_sum(feature_full, team_index, num_segments=ENV_DEVS * TEAMS)
    message = lowered((team_sums[team_index] - feature_full) * inv_peers)
    pre_act = matmul(features, w_hidden) + matmul(message, w_comm)
    hidden = lowered(jnp.tanh(pre_act))
    logits = matmul(hidden, w_policy)
    raised = jnp.exp(logits)
    totals = lax.optimization_barrier(jnp.sum(raised, axis=-1, keepdims=True))
    probs_all = raised / totals
    log_probs = logits - jnp.log(totals)
    chosen = (actions[:, None] == jnp.arange(ACTIONS, dtype=jnp.int32)[None, :]).astype(jnp.float32)
    log_chosen = lax.optimization_barrier(jnp.sum(chosen * log_probs, axis=-1))
    advantage_mean = jnp.sum(advantages) / AGENTS
    advantage_spread = jnp.sum(advantages * advantages) / AGENTS - advantage_mean * advantage_mean
    scaled_advantage = (advantages - advantage_mean) / jnp.sqrt(advantage_spread + NORM_EPS)
    ratios = jnp.exp(log_chosen - old_logp)
    delta_grad = -ratios * scaled_advantage + KL_WEIGHT * (ratios - 1.0)
    logit_grad = lowered(delta_grad[:, None] * (chosen - probs_all))
    ordering = jnp.argsort(env_of, stable=True)
    inverse = jnp.argsort(ordering, stable=True)
    env_inputs = hidden[ordering].reshape(ENVS, ENV_AGENTS, D)
    env_targets = returns[ordering].reshape(ENVS, ENV_AGENTS)

    def one_env(paired):
        return critic_env(paired[0], paired[1], norm_gain, w_query, w_key, w_value)
    input_grads, normed_all, query_all, key_all = lax.map(one_env, (env_inputs, env_targets))
    critic_grad = input_grads.reshape(AGENTS, D)[inverse]
    normed_flat = normed_all.reshape(AGENTS, D)
    query_flat = query_all.reshape(AGENTS, D)
    key_flat = key_all.reshape(AGENTS, D)
    hidden_grad = matmul(logit_grad, w_policy.T) + critic_grad.astype(jnp.float32)
    hidden_full = hidden.astype(jnp.float32)
    pre_grad = lowered(hidden_grad * (1.0 - hidden_full * hidden_full))
    message_grad = matmul(pre_grad, w_comm.T)
    message_sums = jax.ops.segment_sum(message_grad, team_index, num_segments=ENV_DEVS * TEAMS)
    grad_input = (matmul(pre_grad, w_hidden.T) + (message_sums[team_index] - message_grad) * inv_peers).astype(jnp.bfloat16)
    grad_w_hidden = matmul(features.T, pre_grad)
    grad_w_comm = matmul(message.T, pre_grad)
    grad_w_policy = matmul(hidden.T, logit_grad)
    grad_w_query = matmul(normed_flat.T, query_flat)
    grad_w_key = matmul(normed_flat.T, key_flat)
    return (grad_input, grad_w_hidden, grad_w_comm, grad_w_policy, grad_w_query, grad_w_key)
```

```python
import functools
import math

import jax
import jax.numpy as jnp
from jax import lax
from jax.experimental import pallas as pl
from jax.experimental.pallas import tpu as pltpu
from jax.sharding import PartitionSpec as P

HEADS = 4
TEAMS = 4
ENV_AGENTS = 256
ENV_DEV = 2


KL_WEIGHT = 0.5
NORM_EPS = 1e-05


def matmul(left_side, right_side):
    return jnp.dot(left_side, right_side, preferred_element_type=jnp.float32)


def times_trans(left_side, right_side):
    return lax.dot_general(
        left_side, right_side, (((1,), (1,)), ((), ())), preferred_element_type=jnp.float32
    )


def trans_times(left_side, right_side):
    return lax.dot_general(
        left_side, right_side, (((0,), (0,)), ((), ())), preferred_element_type=jnp.float32
    )


def normalize(values):
    center = values - jnp.mean(values, axis=-1, keepdims=True)
    spread = jnp.sqrt(jnp.mean(center * center, axis=-1, keepdims=True) + NORM_EPS)
    return (center / spread, spread)


def normalize_back(gradient, normed, spread):
    mean_grad = jnp.mean(gradient, axis=-1, keepdims=True)
    mean_along = jnp.mean(gradient * normed, axis=-1, keepdims=True)
    return (gradient - mean_grad - normed * mean_along) / spread


def critic_math(rows_of, targets_of, gain, w_query, w_key, w_value, grad_to, wgrad_ref):
    width = w_query.shape[0]
    head_width = width // HEADS
    factor = 1.0 / math.sqrt(head_width)
    totals = [None, None]
    for item in range(ENV_DEV):
        rows_in = rows_of(item).astype(jnp.float32)
        input_hat, input_spread = normalize(rows_in)
        normed = (input_hat * gain).astype(jnp.bfloat16)
        query = matmul(normed, w_query).astype(jnp.bfloat16)
        keys = matmul(normed, w_key).astype(jnp.bfloat16)
        cols = [slice(h * head_width, (h + 1) * head_width) for h in range(HEADS)]
        attention = []
        attended = []
        for c in cols:
            raised = jnp.exp(times_trans(query[:, c], keys[:, c]) * factor)
            attn = raised / jnp.sum(raised, axis=-1, keepdims=True)
            attention.append(attn)
            attended.append(matmul(attn.astype(jnp.bfloat16), normed[:, c]))
        mixed = rows_in + jnp.concatenate(attended, axis=1)
        mixed_hat, mixed_spread = normalize(mixed)
        value_out = jnp.sum(mixed_hat * w_value, axis=-1, keepdims=True)
        value_grad = value_out - targets_of(item)
        mixed_grad = normalize_back(value_grad * w_value, mixed_hat, mixed_spread)
        out_grad = mixed_grad.astype(jnp.bfloat16)
        query_grads = []
        key_grads = []
        sides = []
        for h, c in enumerate(cols):
            attn = attention[h]
            prob_grad = times_trans(out_grad[:, c], normed[:, c])
            sides.append(trans_times(attn.astype(jnp.bfloat16), out_grad[:, c]))
            along = jnp.sum(attn * prob_grad, axis=-1, keepdims=True)
            score_low = (attn * (prob_grad - along) * factor).astype(jnp.bfloat16)
            query_grads.append(matmul(score_low, keys[:, c]).astype(jnp.bfloat16))
            key_grads.append(trans_times(score_low, query[:, c]).astype(jnp.bfloat16))
        query_grad = jnp.concatenate(query_grads, axis=1)
        key_grad = jnp.concatenate(key_grads, axis=1)
        normed_grad = (
            times_trans(query_grad, w_query)
            + times_trans(key_grad, w_key)
            + jnp.concatenate(sides, axis=1)
        )
        back = mixed_grad + normalize_back(normed_grad * gain, input_hat, input_spread)
        grad_to(item, back.astype(jnp.bfloat16))
        for i, grad in enumerate((query_grad, key_grad)):
            part = trans_times(normed, grad)
            totals[i] = part if item == 0 else totals[i] + part
    for i in range(2):
        wgrad_ref[:, i * width : (i + 1) * width] = totals[i].astype(wgrad_ref.dtype)


def critic_kernel(rows_ref, tail_ref, gain_ref, wq_ref, wk_ref, wv_ref, grad_ref, wgrad_ref):
    peers = rows_ref.shape[0]
    width = rows_ref.shape[2]
    per_peer = ENV_AGENTS // peers

    def rows_of(item):
        part = rows_ref[:, item * per_peer : (item + 1) * per_peer, :].astype(jnp.float32)
        return part.reshape(ENV_AGENTS, width)

    def targets_of(item):
        row_id = lax.broadcasted_iota(jnp.int32, (ENV_AGENTS, peers), 0)
        peer_id = lax.broadcasted_iota(jnp.int32, (ENV_AGENTS, peers), 1)
        pick = (row_id // per_peer == peer_id).astype(jnp.bfloat16)
        spread = matmul(pick, tail_ref[:, 0:128])
        row_id = lax.broadcasted_iota(jnp.int32, (ENV_AGENTS, 128), 0)
        lane = lax.broadcasted_iota(jnp.int32, (ENV_AGENTS, 128), 1)
        keep = lane == row_id % per_peer + item * per_peer
        return jnp.sum(jnp.where(keep, spread, 0.0), axis=1, keepdims=True)

    def grad_to(item, value):
        value = value.astype(jnp.float32).reshape(peers, per_peer, width)
        grad_ref[:, item * per_peer : (item + 1) * per_peer, :] = value.astype(jnp.bfloat16)

    critic_math(
        rows_of,
        targets_of,
        gain_ref[...],
        wq_ref[...],
        wk_ref[...],
        wv_ref[...],
        grad_to,
        wgrad_ref,
    )


def critic_call(rows, tail, norm_gain, w_query, w_key, w_value):
    peers = rows.shape[0]
    width = rows.shape[2]
    per_device = ENV_DEV * ENV_AGENTS // peers
    return pl.pallas_call(
        critic_kernel,
        out_shape=(
            jax.ShapeDtypeStruct((peers, per_device, width), jnp.bfloat16),
            jax.ShapeDtypeStruct((width, 2 * width), jnp.bfloat16),
        ),
        in_specs=[pl.BlockSpec(memory_space=pltpu.VMEM)] * 6,
        out_specs=(pl.BlockSpec(memory_space=pltpu.VMEM),) * 2,
        compiler_params=pltpu.CompilerParams(vmem_limit_bytes=48 * 1024 * 1024),
        cost_estimate=pl.CostEstimate(
            flops=6_000_000_000, bytes_accessed=4_000_000, transcendentals=600_000
        ),
    )(rows, tail, norm_gain[None, :], w_query, w_key, w_value[None, :])


def log2(count):
    return count.bit_length() - 1


def scatter_kernel(team_bits, env_bits, orders, *refs):
    count = len(orders)
    stages = team_bits + env_bits
    ins, outs = refs[:count], refs[count : 2 * count]
    refs = refs[2 * count :]
    recv = [refs[i * stages : (i + 1) * stages] for i in range(count)]
    refs = refs[count * stages :]
    sums = [refs[i * (stages - 1) : (i + 1) * (stages - 1)] for i in range(count)]
    refs = refs[count * (stages - 1) :]
    send = [refs[i * (stages - 1) : (i + 1) * (stages - 1)] for i in range(count)]
    send_sem, recv_sem = refs[count * (stages - 1) :]
    team, env = lax.axis_index("team"), lax.axis_index("env")

    def place(bit):
        if bit < team_bits:
            step = 1 << (team_bits - 1 - bit)
            mine = (team // step) % 2
            return mine, (team + (1 - 2 * mine) * step, env)
        step = 1 << (stages - 1 - bit)
        mine = (env // step) % 2
        return mine, (team, env + (1 - 2 * mine) * step)

    places = [place(bit) for bit in range(stages)]
    barrier = pltpu.get_barrier_semaphore()
    for _, peer in places:
        pl.semaphore_signal(barrier, inc=1, device_id=peer, device_id_type=pl.DeviceIdType.MESH)
    pl.semaphore_wait(barrier, stages)

    def start(i, stage):
        bit = orders[i][stage]
        axis = sum(1 for b in range(bit) if b not in orders[i][:stage])
        mine, peer = places[bit]
        before = (slice(None),) * axis
        if stage == 0:
            source = ins[i].at[before + (1 - mine,)]
        else:
            source = send[i][stage - 1]
            source[...] = sums[i][stage - 1][before + (1 - mine,)].astype(jnp.bfloat16)
        copy = pltpu.make_async_remote_copy(
            src_ref=source,
            dst_ref=recv[i][stage],
            send_sem=send_sem.at[i, stage],
            recv_sem=recv_sem.at[i, stage],
            device_id=peer,
            device_id_type=pl.DeviceIdType.MESH,
        )
        copy.start()
        return copy, before + (mine,)

    flight = [start(i, 0) for i in range(count)]
    for stage in range(stages):
        for i in range(count):
            copy, kept = flight[i]
            copy.wait()
            held = ins[i] if stage == 0 else sums[i][stage - 1]
            total = held[kept].astype(jnp.float32) + recv[i][stage][...].astype(jnp.float32)
            if stage == stages - 1:
                outs[i][...] = total
            else:
                sums[i][stage][...] = total
                flight[i] = start(i, stage + 1)


def scatter_sums(parts, team_devs, env_devs):
    team_bits, env_bits = log2(team_devs), log2(env_devs)
    stages = team_bits + env_bits
    rows = parts[0].shape[0] // (team_devs * env_devs)
    team_order = list(range(team_bits))[::-1]
    env_order = list(range(team_bits, stages))[::-1]
    first = team_order + env_order
    second = team_order[:1] + env_order + team_order[1:]
    orders = [first, first, second, second][: len(parts)]

    def left(part, stage, dtype):
        return pltpu.VMEM((2,) * (stages - 1 - stage) + (rows, part.shape[1]), dtype)

    scratch = [left(p, s, jnp.bfloat16) for p in parts for s in range(stages)]
    scratch += [left(p, s, jnp.float32) for p in parts for s in range(stages - 1)]
    scratch += [left(p, s + 1, jnp.bfloat16) for p in parts for s in range(stages - 1)]
    scratch += [pltpu.SemaphoreType.DMA((len(parts), stages))] * 2
    return pl.pallas_call(
        functools.partial(scatter_kernel, team_bits, env_bits, orders),
        out_shape=tuple(jax.ShapeDtypeStruct((rows, p.shape[1]), jnp.float32) for p in parts),
        in_specs=[pl.BlockSpec(memory_space=pltpu.VMEM)] * len(parts),
        out_specs=(pl.BlockSpec(memory_space=pltpu.VMEM),) * len(parts),
        scratch_shapes=scratch,
        compiler_params=pltpu.CompilerParams(
            collective_id=0, has_side_effects=True, vmem_limit_bytes=40 * 1024 * 1024
        ),
        cost_estimate=pl.CostEstimate(flops=5_000_000, bytes_accessed=8_000_000, transcendentals=0),
    )(*[p.reshape((2,) * stages + (rows, p.shape[1])) for p in parts])


def split_three(value):
    high = lax.reduce_precision(value, 8, 7)
    rest = value - high
    middle = lax.reduce_precision(rest, 8, 7)
    low = lax.reduce_precision(rest - middle, 8, 7)
    return [high, middle, low]


def body(
    features,
    team_of,
    env_of,
    actions,
    old_logp,
    advantages,
    returns,
    w_hidden,
    w_comm,
    w_policy,
    norm_gain,
    w_query,
    w_key,
    w_value,
):
    agent_rows, model_width = features.shape
    policy_width = w_policy.shape[1]
    team_devs = lax.axis_size("team")
    env_devs = lax.axis_size("env")
    devices_all = team_devs * env_devs
    members = team_devs * agent_rows // TEAMS
    inv_peers = 1.0 / (members - 1)
    team_mask = team_of[:, None] == jnp.arange(TEAMS, dtype=jnp.int32)[None, :]
    team_low = team_mask.astype(jnp.bfloat16)
    team_full = team_mask.astype(jnp.float32)
    own_sums = jnp.stack([jnp.sum(advantages), jnp.sum(advantages * advantages)])
    own_sums = jnp.pad(own_sums, (0, model_width - 2))[None, :]
    first_sums = lax.psum(
        jnp.concatenate([trans_times(team_low, features), own_sums], axis=0), "team"
    )
    team_sums = first_sums[:TEAMS]
    team_share = jnp.dot(
        team_full, team_sums, precision=lax.Precision.HIGHEST, preferred_element_type=jnp.float32
    )
    message = ((team_share - features.astype(jnp.float32)) * inv_peers).astype(jnp.bfloat16)
    pre_act = matmul(features, w_hidden) + matmul(message, w_comm)
    hidden = jnp.tanh(pre_act).astype(jnp.bfloat16)
    logits = matmul(hidden, w_policy)
    raised = jnp.exp(logits)
    totals = jnp.sum(raised, axis=-1, keepdims=True)
    probs_all = raised / totals
    log_probs = logits - jnp.log(totals)
    chosen = (actions[:, None] == jnp.arange(policy_width, dtype=jnp.int32)[None, :]).astype(
        jnp.float32
    )
    log_chosen = jnp.sum(chosen * log_probs, axis=-1)
    per_peer = ENV_AGENTS // env_devs
    target_device = env_of // ENV_DEV % env_devs
    target_env = env_of % ENV_DEV
    key = target_device * ENV_DEV + target_env
    key_mask = (key[:, None] == jnp.arange(ENV_DEV * env_devs, dtype=jnp.int32)[None, :]).astype(
        jnp.bfloat16
    )
    counter = jnp.arange(agent_rows, dtype=jnp.int32)
    earlier = (counter[:, None] > counter[None, :]).astype(jnp.bfloat16)
    ranks = matmul(earlier, key_mask)
    rank = jnp.sum(ranks * key_mask.astype(jnp.float32), axis=-1).astype(jnp.int32)
    slot = key * per_peer + rank
    placing = (slot[None, :] == counter[:, None]).astype(jnp.bfloat16)
    per_device = ENV_DEV * per_peer
    outgoing = matmul(placing, hidden).astype(jnp.bfloat16)
    outgoing_targets = matmul(placing, returns[:, None]).astype(jnp.bfloat16)
    outgoing_targets = outgoing_targets.reshape(env_devs, per_device)
    pieces = split_three(first_sums[TEAMS, 0]) + split_three(first_sums[TEAMS, 1])
    sent_sums = jnp.broadcast_to(jnp.stack(pieces).astype(jnp.bfloat16)[None, :], (env_devs, 6))
    tail = jnp.concatenate([outgoing_targets, sent_sums], axis=1)
    tail = jnp.pad(tail, ((0, 0), (0, model_width - tail.shape[1])))
    tail = jnp.pad(tail[:, None, :], ((0, 0), (0, 15), (0, 0)))
    arriving = lax.all_to_all(
        jnp.concatenate([outgoing.reshape(env_devs, per_device, model_width), tail], axis=1),
        "env",
        split_axis=0,
        concat_axis=0,
        tiled=True,
    )
    arrived_tail = arriving[:, per_device, :]
    arrived_sums = jnp.sum(
        arrived_tail[:, per_device : per_device + 6].astype(jnp.float32), axis=0
    )
    advantage_total = jnp.sum(arrived_sums[:3])
    advantage_squares = jnp.sum(arrived_sums[3:])
    agent_total = agent_rows * devices_all
    advantage_mean = advantage_total / agent_total
    advantage_spread = advantage_squares / agent_total - advantage_mean * advantage_mean
    scaled_advantage = (advantages - advantage_mean) / jnp.sqrt(advantage_spread + NORM_EPS)
    ratios = jnp.exp(log_chosen - old_logp)
    delta_grad = -ratios * scaled_advantage + KL_WEIGHT * (ratios - 1.0)
    logit_grad = (delta_grad[:, None] * (chosen - probs_all)).astype(jnp.bfloat16)
    input_grad, critic_parts = critic_call(
        arriving, arrived_tail, norm_gain, w_query, w_key, w_value
    )
    returned = lax.all_to_all(input_grad, "env", split_axis=0, concat_axis=0, tiled=True)
    critic_grad = trans_times(placing, returned.reshape(agent_rows, model_width))
    hidden_grad = times_trans(logit_grad, w_policy) + critic_grad
    hidden_full = hidden.astype(jnp.float32)
    pre_grad = (hidden_grad * (1.0 - hidden_full * hidden_full)).astype(jnp.bfloat16)
    message_grad = times_trans(pre_grad, w_comm)
    local_message = lax.dot_general(
        team_full,
        message_grad,
        (((0,), (0,)), ((), ())),
        precision=lax.Precision.HIGHEST,
        preferred_element_type=jnp.float32,
    )
    message_sums = lax.psum(local_message, "team")
    message_share = jnp.dot(
        team_full, message_sums, precision=lax.Precision.HIGHEST, preferred_element_type=jnp.float32
    )
    grad_input = (
        times_trans(pre_grad, w_hidden) + (message_share - message_grad) * inv_peers
    ).astype(jnp.bfloat16)
    parts = [
        trans_times(features, pre_grad).astype(jnp.bfloat16),
        trans_times(message, pre_grad).astype(jnp.bfloat16),
        trans_times(hidden, logit_grad).astype(jnp.bfloat16),
        critic_parts,
    ]
    if model_width // devices_all % 16 == 0:
        summed = scatter_sums(parts, team_devs, env_devs)
    else:
        summed = [
            lax.psum_scatter(
                p.astype(jnp.float32), ("team", "env"), scatter_dimension=0, tiled=True
            )
            for p in parts
        ]
    grad_w_hidden, grad_w_comm, grad_w_policy, critic_sums = summed
    grad_w_query = critic_sums[:, :model_width]
    grad_w_key = critic_sums[:, model_width:]
    return (grad_input, grad_w_hidden, grad_w_comm, grad_w_policy, grad_w_query, grad_w_key)


def solution(mesh):
    in_specs = (
        P(("team", "env"), None),
        P(("team", "env")),
        P(("team", "env")),
        P(("team", "env")),
        P(("team", "env")),
        P(("team", "env")),
        P(("team", "env")),
        P(),
        P(),
        P(),
        P(),
        P(),
        P(),
        P(),
    )
    out_specs = (
        P(("team", "env"), None),
        P(("team", "env"), None),
        P(("team", "env"), None),
        P(("team", "env"), None),
        P(("team", "env"), None),
        P(("team", "env"), None),
    )
    return jax.shard_map(body, mesh=mesh, in_specs=in_specs, out_specs=out_specs, check_vma=False)
```

```python
import functools
import math

import jax
import jax.numpy as jnp
from jax import lax
from jax.experimental import pallas as pl
from jax.experimental.pallas import tpu as pltpu
from jax.sharding import PartitionSpec as P

HEADS = 4
TEAMS = 4
ENV_AGENTS = 256
ENV_DEV = 2


KL_WEIGHT = 0.5
NORM_EPS = 1e-05


def matmul(left_side, right_side):
    return jnp.dot(left_side, right_side, preferred_element_type=jnp.float32)


def times_trans(left_side, right_side):
    return lax.dot_general(
        left_side, right_side, (((1,), (1,)), ((), ())), preferred_element_type=jnp.float32
    )


def trans_times(left_side, right_side):
    return lax.dot_general(
        left_side, right_side, (((0,), (0,)), ((), ())), preferred_element_type=jnp.float32
    )


def normalize(values):
    center = values - jnp.mean(values, axis=-1, keepdims=True)
    spread = jnp.sqrt(jnp.mean(center * center, axis=-1, keepdims=True) + NORM_EPS)
    return (center / spread, spread)


def normalize_back(gradient, normed, spread):
    mean_grad = jnp.mean(gradient, axis=-1, keepdims=True)
    mean_along = jnp.mean(gradient * normed, axis=-1, keepdims=True)
    return (gradient - mean_grad - normed * mean_along) / spread


def log2(count):
    return count.bit_length() - 1


def critic_item(rows_in, targets, gain, w_query, w_key, w_value):
    width = w_query.shape[0]
    head_width = width // HEADS
    factor = 1.0 / math.sqrt(head_width)
    input_hat, input_spread = normalize(rows_in)
    normed = (input_hat * gain).astype(jnp.bfloat16)
    query = matmul(normed, w_query).astype(jnp.bfloat16)
    keys = matmul(normed, w_key).astype(jnp.bfloat16)
    cols = [slice(h * head_width, (h + 1) * head_width) for h in range(HEADS)]
    attention = []
    attended = []
    for c in cols:
        raised = jnp.exp(times_trans(query[:, c], keys[:, c]) * factor)
        attn = raised / jnp.sum(raised, axis=-1, keepdims=True)
        attention.append(attn)
        attended.append(matmul(attn.astype(jnp.bfloat16), normed[:, c]))
    mixed = rows_in + jnp.concatenate(attended, axis=1)
    mixed_hat, mixed_spread = normalize(mixed)
    value_out = jnp.sum(mixed_hat * w_value, axis=-1, keepdims=True)
    value_grad = value_out - targets
    mixed_grad = normalize_back(value_grad * w_value, mixed_hat, mixed_spread)
    out_grad = mixed_grad.astype(jnp.bfloat16)
    query_grads = []
    key_grads = []
    sides = []
    for h, c in enumerate(cols):
        attn = attention[h]
        prob_grad = times_trans(out_grad[:, c], normed[:, c])
        sides.append(trans_times(attn.astype(jnp.bfloat16), out_grad[:, c]))
        along = jnp.sum(attn * prob_grad, axis=-1, keepdims=True)
        score_low = (attn * (prob_grad - along) * factor).astype(jnp.bfloat16)
        query_grads.append(matmul(score_low, keys[:, c]).astype(jnp.bfloat16))
        key_grads.append(trans_times(score_low, query[:, c]).astype(jnp.bfloat16))
    query_grad = jnp.concatenate(query_grads, axis=1)
    key_grad = jnp.concatenate(key_grads, axis=1)
    normed_grad = (
        times_trans(query_grad, w_query)
        + times_trans(key_grad, w_key)
        + jnp.concatenate(sides, axis=1)
    )
    back = mixed_grad + normalize_back(normed_grad * gain, input_hat, input_spread)
    return back.astype(jnp.bfloat16), normed, query_grad, key_grad


def window_kernel(team_devs, env_devs, orders, scatter, *refs):
    team_bits, env_bits = log2(team_devs), log2(env_devs)
    stages = team_bits + env_bits
    (feat_ref, lane_ref, col_ref, wh_ref, wc_ref, wp_ref, gain_ref, wq_ref, wk_ref, wv_ref) = refs[:10]
    out_ref, outs = refs[10], refs[11:15]
    refs = refs[15:]
    (team_send, team_recv, msg_send, msg_recv, rows_send, rows_recv) = refs[:6]
    (tail_send, tail_recv, back_send, back_recv) = refs[6:10]
    (team_ss, team_rs, msg_ss, msg_rs, rows_ss, rows_rs) = refs[10:16]
    (tail_ss, tail_rs, back_ss, back_rs) = refs[16:20]
    refs = refs[20:]
    count = len(orders)
    if scatter:
        ins = refs[:count]
        refs = refs[count:]
        recv = [refs[i * stages : (i + 1) * stages] for i in range(count)]
        refs = refs[count * stages :]
        sums = [refs[i * (stages - 1) : (i + 1) * (stages - 1)] for i in range(count)]
        refs = refs[count * (stages - 1) :]
        send = [refs[i * (stages - 1) : (i + 1) * (stages - 1)] for i in range(count)]
        send_sem, recv_sem = refs[count * (stages - 1) :]
    agents, width = feat_ref.shape
    actions_all = wp_ref.shape[1]
    per_peer = ENV_AGENTS // env_devs
    per_device = ENV_DEV * per_peer
    inv_peers = 1.0 / (team_devs * agents // TEAMS - 1)
    agent_total = agents * team_devs * env_devs
    team, env = lax.axis_index("team"), lax.axis_index("env")
    mesh_id = pl.DeviceIdType.MESH
    team_peers = [((team + d) % team_devs, env) for d in range(1, team_devs)]
    env_peers = [(team, (env + d) % env_devs) for d in range(1, env_devs)]

    barrier = pltpu.get_barrier_semaphore()
    for peer in team_peers + env_peers:
        pl.semaphore_signal(barrier, inc=1, device_id=peer, device_id_type=mesh_id)

    def remote(source, target, send_one, recv_one, peer):
        copy = pltpu.make_async_remote_copy(
            src_ref=source,
            dst_ref=target,
            send_sem=send_one,
            recv_sem=recv_one,
            device_id=peer,
            device_id_type=mesh_id,
        )
        copy.start()
        return copy

    def iota(shape, dim):
        return lax.broadcasted_iota(jnp.int32, shape, dim)

    def team_exchange(source, target, send_one, recv_one):
        return [
            remote(source, target.at[d], send_one.at[d], recv_one.at[d], peer)
            for d, peer in enumerate(team_peers)
        ]

    def team_total(copies, source, target):
        total = source[...]
        for d, copy in enumerate(copies):
            copy.wait()
            total = total + target[d]
        return total

    team_col = col_ref[:, 0:1]

    def share(sums_all):
        total = jnp.where(team_col == 0.0, sums_all[0:1, :], 0.0)
        for t in range(1, TEAMS):
            total = jnp.where(team_col == float(t), sums_all[t : t + 1, :], total)
        return total

    features = feat_ref[...]
    team_row = lane_ref[0:1, :]
    sub = iota((8, agents), 0)
    mask_row = (sub.astype(jnp.float32) == team_row) & (sub < TEAMS)
    team_low = jnp.where(mask_row, 1.0, 0.0).astype(jnp.bfloat16)
    adv_row = lane_ref[3:4, :]
    adv_sum = jnp.sum(adv_row, axis=1, keepdims=True)
    adv_squares = jnp.sum(adv_row * adv_row, axis=1, keepdims=True)
    sub = iota((8, width), 0)
    part = matmul(team_low, features)
    part = jnp.where(sub == TEAMS, adv_sum, part)
    team_send[...] = jnp.where(sub == TEAMS + 1, adv_squares, part)
    pl.semaphore_wait(barrier, len(team_peers) + len(env_peers))
    flight = team_exchange(team_send, team_recv, team_ss, team_rs)

    own_part = matmul(features, wh_ref[...])
    env_row = lane_ref[1:2, :].astype(jnp.int32)
    key_row = (env_row // ENV_DEV % env_devs) * ENV_DEV + env_row % ENV_DEV
    keys_all = ENV_DEV * env_devs
    key_mask = jnp.where(iota((keys_all, agents), 0) == key_row, 1.0, 0.0)
    earlier = jnp.where(iota((agents, agents), 0) < iota((agents, agents), 1), 1.0, 0.0)
    ranks = matmul(key_mask.astype(jnp.bfloat16), earlier.astype(jnp.bfloat16))
    rank = jnp.sum(ranks * key_mask, axis=0, keepdims=True)
    slot = key_row * per_peer + rank.astype(jnp.int32)
    placing = jnp.where(iota((agents, agents), 0) == slot, 1.0, 0.0).astype(jnp.bfloat16)
    returns_row = jnp.broadcast_to(lane_ref[2:3, :], (8, agents)).astype(jnp.bfloat16)
    targets_row = times_trans(returns_row, placing)

    team_sums = team_total(flight, team_send, team_recv)
    sub = iota((8, agents), 0)
    tail = jnp.where(sub == 1, team_sums[TEAMS : TEAMS + 1, 0:1], targets_row)
    tail_send[...] = jnp.where(sub == 2, team_sums[TEAMS + 1 : TEAMS + 2, 0:1], tail)
    tail_recv[env] = tail_send[...]
    tail_flight = [
        remote(tail_send, tail_recv.at[env], tail_ss.at[d], tail_rs.at[d], peer)
        for d, peer in enumerate(env_peers)
    ]
    message = ((share(team_sums) - features.astype(jnp.float32)) * inv_peers).astype(jnp.bfloat16)
    hidden = jnp.tanh(own_part + matmul(message, wc_ref[...])).astype(jnp.bfloat16)
    outgoing = matmul(placing, hidden).reshape(env_devs, per_device, width)
    rows_send[...] = outgoing.astype(jnp.bfloat16)
    rows_recv[env] = rows_send[env]
    rows_flight = [
        remote(rows_send.at[peer[1]], rows_recv.at[env], rows_ss.at[d], rows_rs.at[d], peer)
        for d, peer in enumerate(env_peers)
    ]

    logits = matmul(hidden, wp_ref[...])
    raised = jnp.exp(logits)
    totals = jnp.sum(raised, axis=-1, keepdims=True)
    probs_all = raised / totals
    log_probs = logits - jnp.log(totals)
    lane = iota((agents, actions_all), 1).astype(jnp.float32)
    chosen = jnp.where(lane == col_ref[:, 1:2], 1.0, 0.0)
    log_chosen = jnp.sum(chosen * log_probs, axis=-1, keepdims=True)
    ratios = jnp.exp(log_chosen - col_ref[:, 2:3])
    for copy in tail_flight:
        copy.wait()
    adv_total = jnp.sum(tail_recv[:, 1, 0:1], axis=0, keepdims=True)
    adv_total_sq = jnp.sum(tail_recv[:, 2, 0:1], axis=0, keepdims=True)
    adv_mean = adv_total / agent_total
    adv_var = adv_total_sq / agent_total - adv_mean * adv_mean
    scaled = (col_ref[:, 3:4] - adv_mean) / jnp.sqrt(adv_var + NORM_EPS)
    delta_grad = -ratios * scaled + KL_WEIGHT * (ratios - 1.0)
    logit_grad = (delta_grad * (chosen - probs_all)).astype(jnp.bfloat16)
    policy_back = times_trans(logit_grad, wp_ref[...])
    policy_part = trans_times(hidden, logit_grad)
    target_rows = tail_recv[:, 0, :].astype(jnp.bfloat16)

    for copy in rows_flight:
        copy.wait()
    kept_items = []
    for item in range(ENV_DEV):
        here = slice(item * per_peer, (item + 1) * per_peer)
        rows_in = rows_recv[:, here, :].astype(jnp.float32).reshape(ENV_AGENTS, width)
        row_id = iota((ENV_AGENTS, env_devs), 0)
        pick = jnp.where(row_id // per_peer == iota((ENV_AGENTS, env_devs), 1), 1.0, 0.0)
        spread = matmul(pick.astype(jnp.bfloat16), target_rows)
        wanted = iota((ENV_AGENTS, agents), 0) % per_peer + item * per_peer + env * per_device
        keep = iota((ENV_AGENTS, agents), 1) == wanted
        targets = jnp.sum(jnp.where(keep, spread, 0.0), axis=1, keepdims=True)
        back, *kept = critic_item(
            rows_in, targets, gain_ref[...], wq_ref[...], wk_ref[...], wv_ref[...]
        )
        back = back.astype(jnp.float32).reshape(env_devs, per_peer, width)
        back_send[:, here, :] = back.astype(jnp.bfloat16)
        kept_items.append(kept)
    back_recv[env] = back_send[env]
    back_flight = [
        remote(back_send.at[peer[1]], back_recv.at[env], back_ss.at[d], back_rs.at[d], peer)
        for d, peer in enumerate(env_peers)
    ]

    def place(bit):
        if bit < team_bits:
            step = 1 << (team_bits - 1 - bit)
            mine = (team // step) % 2
            return mine, (team + (1 - 2 * mine) * step, env)
        step = 1 << (stages - 1 - bit)
        mine = (env // step) % 2
        return mine, (team, env + (1 - 2 * mine) * step)

    places = [place(bit) for bit in range(stages)]

    def start(i, stage):
        bit = orders[i][stage]
        axis = sum(1 for b in range(bit) if b not in orders[i][:stage])
        mine, peer = places[bit]
        before = (slice(None),) * axis
        if stage == 0:
            source = ins[i].at[before + (1 - mine,)]
        else:
            source = send[i][stage - 1]
            source[...] = sums[i][stage - 1][before + (1 - mine,)].astype(jnp.bfloat16)
        copy = remote(source, recv[i][stage], send_sem.at[i, stage], recv_sem.at[i, stage], peer)
        return copy, before + (mine,)

    pending = [None] * count

    def advance(i, stage):
        copy, kept = pending[i]
        copy.wait()
        held = ins[i] if stage == 0 else sums[i][stage - 1]
        total = held[kept].astype(jnp.float32) + recv[i][stage][...].astype(jnp.float32)
        if stage == stages - 1:
            outs[i][...] = total
        else:
            sums[i][stage][...] = total
            pending[i] = start(i, stage + 1)

    def emit(i, values):
        if not scatter:
            at = 0
            for value in values:
                outs[i][:, at : at + value.shape[1]] = value.astype(jnp.bfloat16)
                at += value.shape[1]
            return
        at = 0
        for value in values:
            cut = value.reshape(ins[i].shape[:-1] + (value.shape[1],)).astype(jnp.bfloat16)
            ins[i][..., at : at + value.shape[1]] = cut
            at += value.shape[1]
        pending[i] = start(i, 0)

    critic_parts = []
    for which in (1, 2):
        total = trans_times(kept_items[0][0], kept_items[0][which])
        for kept in kept_items[1:]:
            total = total + trans_times(kept[0], kept[which])
        critic_parts.append(total)
    emit(3, critic_parts)
    emit(2, [policy_part])

    for copy in back_flight:
        copy.wait()
    critic_grad = trans_times(placing, back_recv[...].reshape(agents, width))
    hidden_full = hidden.astype(jnp.float32)
    pre_grad = (policy_back + critic_grad) * (1.0 - hidden_full * hidden_full)
    pre_grad = pre_grad.astype(jnp.bfloat16)
    message_grad = times_trans(pre_grad, wc_ref[...])
    msg_send[...] = jnp.dot(
        team_low.astype(jnp.float32),
        message_grad,
        precision=lax.Precision.HIGHEST,
        preferred_element_type=jnp.float32,
    )
    flight = team_exchange(msg_send, msg_recv, msg_ss, msg_rs)
    emit(0, [trans_times(features, pre_grad)])
    emit(1, [trans_times(message, pre_grad)])
    if scatter:
        advance(3, 0)
        advance(2, 0)
    base = times_trans(pre_grad, wh_ref[...])
    message_sums = team_total(flight, msg_send, msg_recv)
    out_ref[...] = (base + (share(message_sums) - message_grad) * inv_peers).astype(jnp.bfloat16)
    if scatter:
        for stage in range(1, stages):
            for i in (0, 1):
                advance(i, stage - 1)
            for i in (3, 2):
                advance(i, stage)
        for i in (0, 1):
            advance(i, stages - 1)


def body(
    features,
    team_of,
    env_of,
    actions,
    old_logp,
    advantages,
    returns,
    w_hidden,
    w_comm,
    w_policy,
    norm_gain,
    w_query,
    w_key,
    w_value,
):
    agents, width = features.shape
    team_devs, env_devs = lax.axis_size("team"), lax.axis_size("env")
    devices = team_devs * env_devs
    team_bits, env_bits = log2(team_devs), log2(env_devs)
    stages = team_bits + env_bits
    full = jnp.float32
    zero = jnp.zeros_like(advantages)
    lanes = [team_of.astype(full), env_of.astype(full), returns.astype(full), advantages]
    lanes = jnp.stack(lanes + [zero] * 4, axis=0)
    columns = jnp.stack(
        [team_of.astype(full), actions.astype(full), old_logp, advantages] + [zero] * 4, axis=1
    )
    rows = width // devices
    scatter = width % devices == 0 and rows % 16 == 0
    widths = [width, width, w_policy.shape[1], 2 * width]
    team_order = list(range(team_bits))[::-1]
    env_order = list(range(team_bits, stages))[::-1]
    first = team_order + env_order
    second = team_order[:1] + env_order + team_order[1:]
    orders = [first, first, second, second]
    per_device = ENV_DEV * ENV_AGENTS // env_devs
    low = jnp.bfloat16
    dma = pltpu.SemaphoreType.DMA

    def both(shape, dtype, copies):
        return [pltpu.VMEM(shape, dtype), pltpu.VMEM((copies,) + shape, dtype)]

    trade = (env_devs, per_device, width)
    scratch = both((8, width), full, team_devs - 1) * 2
    scratch += [pltpu.VMEM(trade, low)] * 2
    scratch += both((8, agents), full, env_devs)
    scratch += [pltpu.VMEM(trade, low)] * 2
    scratch += [dma((team_devs - 1,))] * 4 + [dma((env_devs - 1,))] * 6
    if scatter:

        def left(columns_in, stage, dtype):
            return pltpu.VMEM((2,) * (stages - 1 - stage) + (rows, columns_in), dtype)

        scratch += [left(c, -1, low) for c in widths]
        scratch += [left(c, s, low) for c in widths for s in range(stages)]
        scratch += [left(c, s, full) for c in widths for s in range(stages - 1)]
        scratch += [left(c, s + 1, low) for c in widths for s in range(stages - 1)]
        scratch += [dma((len(widths), stages))] * 2
        out_parts = tuple(jax.ShapeDtypeStruct((rows, c), full) for c in widths)
    else:
        out_parts = tuple(jax.ShapeDtypeStruct((width, c), low) for c in widths)
    grad_input, *parts = pl.pallas_call(
        functools.partial(window_kernel, team_devs, env_devs, orders, scatter),
        out_shape=(jax.ShapeDtypeStruct((agents, width), low),) + out_parts,
        in_specs=[pl.BlockSpec(memory_space=pltpu.VMEM)] * 10,
        out_specs=(pl.BlockSpec(memory_space=pltpu.VMEM),) * 5,
        scratch_shapes=scratch,
        compiler_params=pltpu.CompilerParams(
            collective_id=0, has_side_effects=True, vmem_limit_bytes=52 * 1024 * 1024
        ),
        cost_estimate=pl.CostEstimate(
            flops=11_000_000_000, bytes_accessed=6_000_000, transcendentals=1_000_000
        ),
    )(
        features,
        lanes,
        columns,
        w_hidden,
        w_comm,
        w_policy,
        norm_gain[None, :],
        w_query,
        w_key,
        w_value[None, :],
    )
    if not scatter:
        parts = [
            lax.psum_scatter(p.astype(full), ("team", "env"), scatter_dimension=0, tiled=True)
            for p in parts
        ]
    grad_w_hidden, grad_w_comm, grad_w_policy, critic_sums = parts
    return (
        grad_input,
        grad_w_hidden,
        grad_w_comm,
        grad_w_policy,
        critic_sums[:, :width],
        critic_sums[:, width:],
    )


def solution(mesh):
    in_specs = (
        P(("team", "env"), None),
        P(("team", "env")),
        P(("team", "env")),
        P(("team", "env")),
        P(("team", "env")),
        P(("team", "env")),
        P(("team", "env")),
        P(),
        P(),
        P(),
        P(),
        P(),
        P(),
        P(),
    )
    out_specs = (
        P(("team", "env"), None),
        P(("team", "env"), None),
        P(("team", "env"), None),
        P(("team", "env"), None),
        P(("team", "env"), None),
        P(("team", "env"), None),
    )
    return jax.shard_map(body, mesh=mesh, in_specs=in_specs, out_specs=out_specs, check_vma=False)
```

```python
import functools
import math

import jax
import jax.numpy as jnp
from jax import lax
from jax.experimental import pallas as pl
from jax.experimental.pallas import tpu as pltpu
from jax.sharding import PartitionSpec as P

HEADS = 4
TEAMS = 4
ENV_AGENTS = 256
ENV_DEV = 2


KL_WEIGHT = 0.5
NORM_EPS = 1e-05


def matmul(left_side, right_side):
    return jnp.dot(left_side, right_side, preferred_element_type=jnp.float32)


def times_trans(left_side, right_side):
    return lax.dot_general(
        left_side, right_side, (((1,), (1,)), ((), ())), preferred_element_type=jnp.float32
    )


def trans_times(left_side, right_side):
    return lax.dot_general(
        left_side, right_side, (((0,), (0,)), ((), ())), preferred_element_type=jnp.float32
    )


def normalize(values):
    center = values - jnp.mean(values, axis=-1, keepdims=True)
    spread = jnp.sqrt(jnp.mean(center * center, axis=-1, keepdims=True) + NORM_EPS)
    return (center / spread, spread)


def normalize_back(gradient, normed, spread):
    mean_grad = jnp.mean(gradient, axis=-1, keepdims=True)
    mean_along = jnp.mean(gradient * normed, axis=-1, keepdims=True)
    return (gradient - mean_grad - normed * mean_along) / spread


def log2(count):
    return count.bit_length() - 1


def critic_item(rows_in, targets, gain, w_query, w_key, w_value):
    width = w_query.shape[0]
    head_width = width // HEADS
    factor = 1.0 / math.sqrt(head_width)
    input_hat, input_spread = normalize(rows_in)
    normed = (input_hat * gain).astype(jnp.bfloat16)
    query = matmul(normed, w_query).astype(jnp.bfloat16)
    keys = matmul(normed, w_key).astype(jnp.bfloat16)
    cols = [slice(h * head_width, (h + 1) * head_width) for h in range(HEADS)]
    attention = []
    attended = []
    for c in cols:
        raised = jnp.exp(times_trans(query[:, c], keys[:, c]) * factor)
        attn = raised / jnp.sum(raised, axis=-1, keepdims=True)
        attention.append(attn)
        attended.append(matmul(attn.astype(jnp.bfloat16), normed[:, c]))
    mixed = rows_in + jnp.concatenate(attended, axis=1)
    mixed_hat, mixed_spread = normalize(mixed)
    value_out = jnp.sum(mixed_hat * w_value, axis=-1, keepdims=True)
    value_grad = value_out - targets
    mixed_grad = normalize_back(value_grad * w_value, mixed_hat, mixed_spread)
    out_grad = mixed_grad.astype(jnp.bfloat16)
    query_grads = []
    key_grads = []
    sides = []
    for h, c in enumerate(cols):
        attn = attention[h]
        prob_grad = times_trans(out_grad[:, c], normed[:, c])
        sides.append(trans_times(attn.astype(jnp.bfloat16), out_grad[:, c]))
        along = jnp.sum(attn * prob_grad, axis=-1, keepdims=True)
        score_low = (attn * (prob_grad - along) * factor).astype(jnp.bfloat16)
        query_grads.append(matmul(score_low, keys[:, c]).astype(jnp.bfloat16))
        key_grads.append(trans_times(score_low, query[:, c]).astype(jnp.bfloat16))
    query_grad = jnp.concatenate(query_grads, axis=1)
    key_grad = jnp.concatenate(key_grads, axis=1)
    normed_grad = (
        times_trans(query_grad, w_query)
        + times_trans(key_grad, w_key)
        + jnp.concatenate(sides, axis=1)
    )
    back = mixed_grad + normalize_back(normed_grad * gain, input_hat, input_spread)
    return back.astype(jnp.bfloat16), normed, query_grad, key_grad


def window_kernel(team_devs, env_devs, orders, scatter, *refs):
    team_bits, env_bits = log2(team_devs), log2(env_devs)
    stages = team_bits + env_bits
    feat_ref, wh_ref, wc_ref, wp_ref, gain_ref, wq_ref, wk_ref, wv_ref = refs[:8]
    agent_hbm, out_ref, parts_ref = refs[8:14], refs[14], refs[15]
    agent_refs, agent_sem = refs[16:22], refs[22]
    refs = refs[23:]
    loads = [
        pltpu.make_async_copy(source, target, agent_sem.at[i])
        for i, (source, target) in enumerate(zip(agent_hbm, agent_refs))
    ]
    for load in loads:
        load.start()
    actions_width, model_width = wp_ref.shape[1], wp_ref.shape[0]
    edges = [0, model_width, 2 * model_width, 2 * model_width + actions_width]
    edges.append(edges[-1] + 2 * model_width)
    (team_send, team_recv, msg_send, msg_recv, rows_send, rows_recv) = refs[:6]
    (tail_send, tail_recv, back_send, back_recv) = refs[6:10]
    (team_ss, team_rs, msg_ss, msg_rs, rows_ss, rows_rs) = refs[10:16]
    (tail_ss, tail_rs, back_ss, back_rs) = refs[16:20]
    refs = refs[20:]
    count = len(orders)
    if scatter:
        ins = refs[:count]
        refs = refs[count:]
        recv = [refs[i * stages : (i + 1) * stages] for i in range(count)]
        refs = refs[count * stages :]
        sums = [refs[i * (stages - 1) : (i + 1) * (stages - 1)] for i in range(count)]
        refs = refs[count * (stages - 1) :]
        send = [refs[i * (stages - 1) : (i + 1) * (stages - 1)] for i in range(count)]
        send_sem, recv_sem = refs[count * (stages - 1) :]
    agents, width = feat_ref.shape
    actions_all = wp_ref.shape[1]
    per_peer = ENV_AGENTS // env_devs
    per_device = ENV_DEV * per_peer
    inv_peers = 1.0 / (team_devs * agents // TEAMS - 1)
    agent_total = agents * team_devs * env_devs
    team, env = lax.axis_index("team"), lax.axis_index("env")
    mesh_id = pl.DeviceIdType.MESH
    team_peers = [((team + d) % team_devs, env) for d in range(1, team_devs)]
    env_peers = [(team, (env + d) % env_devs) for d in range(1, env_devs)]

    barrier = pltpu.get_barrier_semaphore()
    for peer in team_peers + env_peers:
        pl.semaphore_signal(barrier, inc=1, device_id=peer, device_id_type=mesh_id)

    def remote(source, target, send_one, recv_one, peer):
        copy = pltpu.make_async_remote_copy(
            src_ref=source,
            dst_ref=target,
            send_sem=send_one,
            recv_sem=recv_one,
            device_id=peer,
            device_id_type=mesh_id,
        )
        copy.start()
        return copy

    def iota(shape, dim):
        return lax.broadcasted_iota(jnp.int32, shape, dim)

    def team_exchange(source, target, send_one, recv_one):
        return [
            remote(source, target.at[d], send_one.at[d], recv_one.at[d], peer)
            for d, peer in enumerate(team_peers)
        ]

    def team_total(copies, source, target):
        total = source[...]
        for d, copy in enumerate(copies):
            copy.wait()
            total = total + target[d]
        return total

    def share(sums_all):
        total = jnp.where(team_col == 0.0, sums_all[0:1, :], 0.0)
        for t in range(1, TEAMS):
            total = jnp.where(team_col == float(t), sums_all[t : t + 1, :], total)
        return total

    for load in loads:
        load.wait()
    team_ref, env_ref, action_ref, logp_ref, adv_ref, returns_ref = agent_refs
    features = feat_ref[...]
    team_row = team_ref[...].astype(jnp.float32)
    sub = iota((8, agents), 0)
    mask_row = (sub.astype(jnp.float32) == team_row) & (sub < TEAMS)
    team_low = jnp.where(mask_row, 1.0, 0.0).astype(jnp.bfloat16)
    adv_row = adv_ref[...]
    adv_sum = jnp.sum(adv_row, axis=1, keepdims=True)
    adv_squares = jnp.sum(adv_row * adv_row, axis=1, keepdims=True)
    sub = iota((8, width), 0)
    part = matmul(team_low, features)
    part = jnp.where(sub == TEAMS, adv_sum, part)
    team_send[...] = jnp.where(sub == TEAMS + 1, adv_squares, part)
    pl.semaphore_wait(barrier, len(team_peers) + len(env_peers))
    flight = team_exchange(team_send, team_recv, team_ss, team_rs)

    diagonal = iota((agents, agents), 0) == iota((agents, agents), 1)

    def column(row):
        return jnp.sum(jnp.where(diagonal, row, 0.0), axis=1, keepdims=True)

    team_col = column(team_row)
    own_part = matmul(features, wh_ref[...])
    env_row = env_ref[...]
    key_row = (env_row // ENV_DEV % env_devs) * ENV_DEV + env_row % ENV_DEV
    keys_all = ENV_DEV * env_devs
    key_mask = jnp.where(iota((keys_all, agents), 0) == key_row, 1.0, 0.0)
    earlier = jnp.where(iota((agents, agents), 0) < iota((agents, agents), 1), 1.0, 0.0)
    ranks = matmul(key_mask.astype(jnp.bfloat16), earlier.astype(jnp.bfloat16))
    rank = jnp.sum(ranks * key_mask, axis=0, keepdims=True)
    slot = key_row * per_peer + rank.astype(jnp.int32)
    placing = jnp.where(iota((agents, agents), 0) == slot, 1.0, 0.0).astype(jnp.bfloat16)
    returns_row = jnp.broadcast_to(returns_ref[...], (8, agents)).astype(jnp.bfloat16)
    targets_row = times_trans(returns_row, placing)

    team_sums = team_total(flight, team_send, team_recv)
    sub = iota((8, agents), 0)
    tail = jnp.where(sub == 1, team_sums[TEAMS : TEAMS + 1, 0:1], targets_row)
    tail_send[...] = jnp.where(sub == 2, team_sums[TEAMS + 1 : TEAMS + 2, 0:1], tail)
    tail_recv[env] = tail_send[...]
    tail_flight = [
        remote(tail_send, tail_recv.at[env], tail_ss.at[d], tail_rs.at[d], peer)
        for d, peer in enumerate(env_peers)
    ]
    message = ((share(team_sums) - features.astype(jnp.float32)) * inv_peers).astype(jnp.bfloat16)
    hidden = jnp.tanh(own_part + matmul(message, wc_ref[...])).astype(jnp.bfloat16)
    outgoing = matmul(placing, hidden).reshape(env_devs, per_device, width)
    rows_send[...] = outgoing.astype(jnp.bfloat16)
    rows_recv[env] = rows_send[env]
    groups = ENV_DEV if per_peer % 16 == 0 else 1
    group_rows = per_device // groups

    def trade(group, source, target, send_one, recv_one):
        here = pl.ds(group * group_rows, group_rows)
        return [
            remote(
                source.at[peer[1], here],
                target.at[env, here],
                send_one.at[group, d],
                recv_one.at[group, d],
                peer,
            )
            for d, peer in enumerate(env_peers)
        ]

    rows_flight = [trade(g, rows_send, rows_recv, rows_ss, rows_rs) for g in range(groups)]

    logits = matmul(hidden, wp_ref[...])
    raised = jnp.exp(logits)
    totals = jnp.sum(raised, axis=-1, keepdims=True)
    probs_all = raised / totals
    log_probs = logits - jnp.log(totals)
    lane = iota((agents, actions_all), 1).astype(jnp.float32)
    chosen = jnp.where(lane == column(action_ref[...].astype(jnp.float32)), 1.0, 0.0)
    log_chosen = jnp.sum(chosen * log_probs, axis=-1, keepdims=True)
    ratios = jnp.exp(log_chosen - column(logp_ref[...]))
    for copy in tail_flight:
        copy.wait()
    adv_total = jnp.sum(tail_recv[:, 1, 0:1], axis=0, keepdims=True)
    adv_total_sq = jnp.sum(tail_recv[:, 2, 0:1], axis=0, keepdims=True)
    adv_mean = adv_total / agent_total
    adv_var = adv_total_sq / agent_total - adv_mean * adv_mean
    scaled = (column(adv_row) - adv_mean) / jnp.sqrt(adv_var + NORM_EPS)
    delta_grad = -ratios * scaled + KL_WEIGHT * (ratios - 1.0)
    logit_grad = (delta_grad * (chosen - probs_all)).astype(jnp.bfloat16)
    policy_back = times_trans(logit_grad, wp_ref[...])
    policy_part = trans_times(hidden, logit_grad)
    target_rows = tail_recv[:, 0, :].astype(jnp.bfloat16)

    kept_items = []
    back_flight = []
    for item in range(ENV_DEV):
        if item < groups:
            for copy in rows_flight[item]:
                copy.wait()
        here = slice(item * per_peer, (item + 1) * per_peer)
        rows_in = rows_recv[:, here, :].astype(jnp.float32).reshape(ENV_AGENTS, width)
        row_id = iota((ENV_AGENTS, env_devs), 0)
        pick = jnp.where(row_id // per_peer == iota((ENV_AGENTS, env_devs), 1), 1.0, 0.0)
        spread = matmul(pick.astype(jnp.bfloat16), target_rows)
        wanted = iota((ENV_AGENTS, agents), 0) % per_peer + item * per_peer + env * per_device
        keep = iota((ENV_AGENTS, agents), 1) == wanted
        targets = jnp.sum(jnp.where(keep, spread, 0.0), axis=1, keepdims=True)
        back, *kept = critic_item(
            rows_in, targets, gain_ref[...], wq_ref[...], wk_ref[...], wv_ref[...]
        )
        back = back.astype(jnp.float32).reshape(env_devs, per_peer, width)
        back_send[:, here, :] = back.astype(jnp.bfloat16)
        kept_items.append(kept)
        if groups > 1 or item == ENV_DEV - 1:
            group = item if groups > 1 else 0
            back_flight += trade(group, back_send, back_recv, back_ss, back_rs)
    back_recv[env] = back_send[env]

    def place(bit):
        if bit < team_bits:
            step = 1 << (team_bits - 1 - bit)
            mine = (team // step) % 2
            return mine, (team + (1 - 2 * mine) * step, env)
        step = 1 << (stages - 1 - bit)
        mine = (env // step) % 2
        return mine, (team, env + (1 - 2 * mine) * step)

    places = [place(bit) for bit in range(stages)]

    def start(i, stage):
        bit = orders[i][stage]
        axis = sum(1 for b in range(bit) if b not in orders[i][:stage])
        mine, peer = places[bit]
        before = (slice(None),) * axis
        if stage == 0:
            source = ins[i].at[before + (1 - mine,)]
        else:
            source = send[i][stage - 1]
            source[...] = sums[i][stage - 1][before + (1 - mine,)].astype(jnp.bfloat16)
        copy = remote(source, recv[i][stage], send_sem.at[i, stage], recv_sem.at[i, stage], peer)
        return copy, before + (mine,)

    pending = [None] * count

    def advance(i, stage):
        copy, kept = pending[i]
        copy.wait()
        held = ins[i] if stage == 0 else sums[i][stage - 1]
        total = held[kept].astype(jnp.float32) + recv[i][stage][...].astype(jnp.float32)
        if stage == stages - 1:
            parts_ref[:, edges[i] : edges[i + 1]] = total
        else:
            sums[i][stage][...] = total
            pending[i] = start(i, stage + 1)

    def emit(i, values):
        if not scatter:
            at = edges[i]
            for value in values:
                parts_ref[:, at : at + value.shape[1]] = value.astype(jnp.bfloat16)
                at += value.shape[1]
            return
        at = 0
        for value in values:
            cut = value.reshape(ins[i].shape[:-1] + (value.shape[1],)).astype(jnp.bfloat16)
            ins[i][..., at : at + value.shape[1]] = cut
            at += value.shape[1]
        pending[i] = start(i, 0)

    critic_parts = []
    for which in (1, 2):
        total = trans_times(kept_items[0][0], kept_items[0][which])
        for kept in kept_items[1:]:
            total = total + trans_times(kept[0], kept[which])
        critic_parts.append(total)
    emit(3, critic_parts)
    emit(2, [policy_part])

    for copy in back_flight:
        copy.wait()
    critic_grad = trans_times(placing, back_recv[...].reshape(agents, width))
    hidden_full = hidden.astype(jnp.float32)
    pre_grad = (policy_back + critic_grad) * (1.0 - hidden_full * hidden_full)
    pre_grad = pre_grad.astype(jnp.bfloat16)
    message_grad = times_trans(pre_grad, wc_ref[...])
    msg_send[...] = jnp.dot(
        team_low.astype(jnp.float32),
        message_grad,
        precision=lax.Precision.HIGHEST,
        preferred_element_type=jnp.float32,
    )
    flight = team_exchange(msg_send, msg_recv, msg_ss, msg_rs)
    emit(0, [trans_times(features, pre_grad)])
    emit(1, [trans_times(message, pre_grad)])
    if scatter:
        advance(3, 0)
        advance(2, 0)
    base = times_trans(pre_grad, wh_ref[...])
    message_sums = team_total(flight, msg_send, msg_recv)
    out_ref[...] = (base + (share(message_sums) - message_grad) * inv_peers).astype(jnp.bfloat16)
    if scatter:
        for stage in range(1, stages):
            for i in (0, 1):
                advance(i, stage - 1)
            for i in (3, 2):
                advance(i, stage)
        for i in (0, 1):
            advance(i, stages - 1)


def body(
    features,
    team_of,
    env_of,
    actions,
    old_logp,
    advantages,
    returns,
    w_hidden,
    w_comm,
    w_policy,
    norm_gain,
    w_query,
    w_key,
    w_value,
):
    agents, width = features.shape
    team_devs, env_devs = lax.axis_size("team"), lax.axis_size("env")
    devices = team_devs * env_devs
    team_bits, env_bits = log2(team_devs), log2(env_devs)
    stages = team_bits + env_bits
    full = jnp.float32
    rows = width // devices
    scatter = width % devices == 0 and rows % 16 == 0
    widths = [width, width, w_policy.shape[1], 2 * width]
    team_order = list(range(team_bits))[::-1]
    env_order = list(range(team_bits, stages))[::-1]
    first = team_order + env_order
    second = team_order[:1] + env_order + team_order[1:]
    orders = [first, first, second, second]
    per_device = ENV_DEV * ENV_AGENTS // env_devs
    low = jnp.bfloat16
    dma = pltpu.SemaphoreType.DMA

    def both(shape, dtype, copies):
        return [pltpu.VMEM(shape, dtype), pltpu.VMEM((copies,) + shape, dtype)]

    trade = (env_devs, per_device, width)
    agent_inputs = [team_of, env_of, actions, old_logp, advantages, returns.astype(full)]
    agent_inputs = [value[None, :] for value in agent_inputs]
    scratch = [pltpu.VMEM(value.shape, value.dtype) for value in agent_inputs]
    scratch += [dma((len(agent_inputs),))]
    scratch += both((8, width), full, team_devs - 1) * 2
    scratch += [pltpu.VMEM(trade, low)] * 2
    scratch += both((8, agents), full, env_devs)
    scratch += [pltpu.VMEM(trade, low)] * 2
    scratch += [dma((team_devs - 1,))] * 4 + [dma((ENV_DEV, env_devs - 1))] * 2
    scratch += [dma((env_devs - 1,))] * 2 + [dma((ENV_DEV, env_devs - 1))] * 2
    if scatter:

        def left(columns_in, stage, dtype):
            return pltpu.VMEM((2,) * (stages - 1 - stage) + (rows, columns_in), dtype)

        scratch += [left(c, -1, low) for c in widths]
        scratch += [left(c, s, low) for c in widths for s in range(stages)]
        scratch += [left(c, s, full) for c in widths for s in range(stages - 1)]
        scratch += [left(c, s + 1, low) for c in widths for s in range(stages - 1)]
        scratch += [dma((len(widths), stages))] * 2
        out_parts = jax.ShapeDtypeStruct((rows, sum(widths)), full)
    else:
        out_parts = jax.ShapeDtypeStruct((width, sum(widths)), low)
    grad_input, parts = pl.pallas_call(
        functools.partial(window_kernel, team_devs, env_devs, orders, scatter),
        out_shape=(jax.ShapeDtypeStruct((agents, width), low), out_parts),
        in_specs=[pl.BlockSpec(memory_space=pltpu.VMEM)] * 8 + [pl.BlockSpec(memory_space=pl.ANY)] * 6,
        out_specs=(pl.BlockSpec(memory_space=pltpu.VMEM),) * 2,
        scratch_shapes=scratch,
        compiler_params=pltpu.CompilerParams(
            collective_id=0, has_side_effects=True, vmem_limit_bytes=60 * 1024 * 1024
        ),
        cost_estimate=pl.CostEstimate(
            flops=11_000_000_000, bytes_accessed=6_000_000, transcendentals=1_000_000
        ),
    )(
        features,
        w_hidden,
        w_comm,
        w_policy,
        norm_gain[None, :],
        w_query,
        w_key,
        w_value[None, :],
        *agent_inputs,
    )
    if not scatter:
        parts = lax.psum_scatter(
            parts.astype(full), ("team", "env"), scatter_dimension=0, tiled=True
        )
    edges = [0]
    for wide in (width, width, w_policy.shape[1], width, width):
        edges.append(edges[-1] + wide)
    return (grad_input, *[parts[:, a:b] for a, b in zip(edges[:-1], edges[1:])])


def solution(mesh):
    in_specs = (
        P(("team", "env"), None),
        P(("team", "env")),
        P(("team", "env")),
        P(("team", "env")),
        P(("team", "env")),
        P(("team", "env")),
        P(("team", "env")),
        P(),
        P(),
        P(),
        P(),
        P(),
        P(),
        P(),
    )
    out_specs = (
        P(("team", "env"), None),
        P(("team", "env"), None),
        P(("team", "env"), None),
        P(("team", "env"), None),
        P(("team", "env"), None),
        P(("team", "env"), None),
    )
    return jax.shard_map(body, mesh=mesh, in_specs=in_specs, out_specs=out_specs, check_vma=False)
```

```python
import functools
import math

import jax
import jax.numpy as jnp
from jax import lax
from jax.experimental import pallas as pl
from jax.experimental.pallas import tpu as pltpu
from jax.sharding import PartitionSpec as P

HEADS = 4
TEAMS = 4
ENV_AGENTS = 256
ENV_DEV = 2


KL_WEIGHT = 0.5
NORM_EPS = 1e-05


def matmul(left_side, right_side):
    return jnp.dot(left_side, right_side, preferred_element_type=jnp.float32)


def times_trans(left_side, right_side):
    return lax.dot_general(
        left_side, right_side, (((1,), (1,)), ((), ())), preferred_element_type=jnp.float32
    )


def trans_times(left_side, right_side):
    return lax.dot_general(
        left_side, right_side, (((0,), (0,)), ((), ())), preferred_element_type=jnp.float32
    )


def normalize(values):
    center = values - jnp.mean(values, axis=-1, keepdims=True)
    spread = jnp.sqrt(jnp.mean(center * center, axis=-1, keepdims=True) + NORM_EPS)
    return (center / spread, spread)


def normalize_back(gradient, normed, spread):
    mean_grad = jnp.mean(gradient, axis=-1, keepdims=True)
    mean_along = jnp.mean(gradient * normed, axis=-1, keepdims=True)
    return (gradient - mean_grad - normed * mean_along) / spread


def log2(count):
    return count.bit_length() - 1


def critic_item(rows_in, targets, gain, w_query, w_key, w_value):
    width = w_query.shape[0]
    head_width = width // HEADS
    factor = 1.0 / math.sqrt(head_width)
    input_hat, input_spread = normalize(rows_in)
    normed = (input_hat * gain).astype(jnp.bfloat16)
    query = matmul(normed, w_query).astype(jnp.bfloat16)
    keys = matmul(normed, w_key).astype(jnp.bfloat16)
    cols = [slice(h * head_width, (h + 1) * head_width) for h in range(HEADS)]
    attention = []
    attended = []
    for c in cols:
        raised = jnp.exp(times_trans(query[:, c], keys[:, c]) * factor)
        attn = raised / jnp.sum(raised, axis=-1, keepdims=True)
        attention.append(attn)
        attended.append(matmul(attn.astype(jnp.bfloat16), normed[:, c]))
    mixed = rows_in + jnp.concatenate(attended, axis=1)
    mixed_hat, mixed_spread = normalize(mixed)
    value_out = jnp.sum(mixed_hat * w_value, axis=-1, keepdims=True)
    value_grad = value_out - targets
    mixed_grad = normalize_back(value_grad * w_value, mixed_hat, mixed_spread)
    out_grad = mixed_grad.astype(jnp.bfloat16)
    query_grads = []
    key_grads = []
    sides = []
    for h, c in enumerate(cols):
        attn = attention[h]
        prob_grad = times_trans(out_grad[:, c], normed[:, c])
        sides.append(trans_times(attn.astype(jnp.bfloat16), out_grad[:, c]))
        along = jnp.sum(attn * prob_grad, axis=-1, keepdims=True)
        score_low = (attn * (prob_grad - along) * factor).astype(jnp.bfloat16)
        query_grads.append(matmul(score_low, keys[:, c]).astype(jnp.bfloat16))
        key_grads.append(trans_times(score_low, query[:, c]).astype(jnp.bfloat16))
    query_grad = jnp.concatenate(query_grads, axis=1)
    key_grad = jnp.concatenate(key_grads, axis=1)
    normed_grad = (
        times_trans(query_grad, w_query)
        + times_trans(key_grad, w_key)
        + jnp.concatenate(sides, axis=1)
    )
    back = mixed_grad + normalize_back(normed_grad * gain, input_hat, input_spread)
    return back.astype(jnp.bfloat16), normed, query_grad, key_grad


def window_kernel(team_devs, env_devs, orders, scatter, *refs):
    team_bits, env_bits = log2(team_devs), log2(env_devs)
    stages = team_bits + env_bits
    agent_hbm, out_ref, parts_ref = refs[:14], refs[14], refs[15]
    agent_refs, agent_sem = refs[16:30], refs[30]
    refs = refs[31:]
    team_ref, env_ref, action_ref, logp_ref, adv_ref, returns_ref, feat_ref = agent_refs[:7]
    wh_ref, wc_ref, wp_ref, gain_ref, wq_ref, wk_ref, wv_ref = agent_refs[7:]
    loads = [
        pltpu.make_async_copy(source, target, agent_sem.at[i])
        for i, (source, target) in enumerate(zip(agent_hbm, agent_refs))
    ]
    for load in loads:
        load.start()
    actions_width, model_width = wp_ref.shape[1], wp_ref.shape[0]
    edges = [0, model_width, 2 * model_width, 2 * model_width + actions_width]
    edges.append(edges[-1] + 2 * model_width)
    (team_send, team_recv, msg_send, msg_recv, rows_send, rows_recv) = refs[:6]
    (tail_send, tail_recv, back_send, back_recv) = refs[6:10]
    (team_ss, team_rs, msg_ss, msg_rs, rows_ss, rows_rs) = refs[10:16]
    (tail_ss, tail_rs, back_ss, back_rs) = refs[16:20]
    refs = refs[20:]
    count = len(orders)
    if scatter:
        ins = refs[:count]
        refs = refs[count:]
        recv = [refs[i * stages : (i + 1) * stages] for i in range(count)]
        refs = refs[count * stages :]
        sums = [refs[i * (stages - 1) : (i + 1) * (stages - 1)] for i in range(count)]
        refs = refs[count * (stages - 1) :]
        send = [refs[i * (stages - 1) : (i + 1) * (stages - 1)] for i in range(count)]
        send_sem, recv_sem = refs[count * (stages - 1) :]
    agents, width = feat_ref.shape
    actions_all = wp_ref.shape[1]
    per_peer = ENV_AGENTS // env_devs
    per_device = ENV_DEV * per_peer
    inv_peers = 1.0 / (team_devs * agents // TEAMS - 1)
    agent_total = agents * team_devs * env_devs
    team, env = lax.axis_index("team"), lax.axis_index("env")
    mesh_id = pl.DeviceIdType.MESH
    team_peers = [((team + d) % team_devs, env) for d in range(1, team_devs)]
    env_peers = [(team, (env + d) % env_devs) for d in range(1, env_devs)]

    barrier = pltpu.get_barrier_semaphore()
    for peer in team_peers + env_peers:
        pl.semaphore_signal(barrier, inc=1, device_id=peer, device_id_type=mesh_id)

    def remote(source, target, send_one, recv_one, peer):
        copy = pltpu.make_async_remote_copy(
            src_ref=source,
            dst_ref=target,
            send_sem=send_one,
            recv_sem=recv_one,
            device_id=peer,
            device_id_type=mesh_id,
        )
        copy.start()
        return copy

    def iota(shape, dim):
        return lax.broadcasted_iota(jnp.int32, shape, dim)

    def team_exchange(source, target, send_one, recv_one):
        return [
            remote(source, target.at[d], send_one.at[d], recv_one.at[d], peer)
            for d, peer in enumerate(team_peers)
        ]

    def team_total(copies, source, target):
        total = source[...]
        for d, copy in enumerate(copies):
            copy.wait()
            total = total + target[d]
        return total

    def share(sums_all):
        total = jnp.where(team_col == 0.0, sums_all[0:1, :], 0.0)
        for t in range(1, TEAMS):
            total = jnp.where(team_col == float(t), sums_all[t : t + 1, :], total)
        return total

    for load in loads[:7]:
        load.wait()
    features = feat_ref[...]
    team_row = team_ref[...].astype(jnp.float32)
    sub = iota((8, agents), 0)
    mask_row = (sub.astype(jnp.float32) == team_row) & (sub < TEAMS)
    team_low = jnp.where(mask_row, 1.0, 0.0).astype(jnp.bfloat16)
    adv_row = adv_ref[...]
    adv_sum = jnp.sum(adv_row, axis=1, keepdims=True)
    adv_squares = jnp.sum(adv_row * adv_row, axis=1, keepdims=True)
    sub = iota((8, width), 0)
    part = matmul(team_low, features)
    part = jnp.where(sub == TEAMS, adv_sum, part)
    team_send[...] = jnp.where(sub == TEAMS + 1, adv_squares, part)
    pl.semaphore_wait(barrier, len(team_peers) + len(env_peers))
    flight = team_exchange(team_send, team_recv, team_ss, team_rs)

    for load in loads[7:]:
        load.wait()
    diagonal = iota((agents, agents), 0) == iota((agents, agents), 1)

    def column(row):
        return jnp.sum(jnp.where(diagonal, row, 0.0), axis=1, keepdims=True)

    team_col = column(team_row)
    own_part = matmul(features, wh_ref[...])
    env_row = env_ref[...]
    key_row = (env_row // ENV_DEV % env_devs) * ENV_DEV + env_row % ENV_DEV
    keys_all = ENV_DEV * env_devs
    key_mask = jnp.where(iota((keys_all, agents), 0) == key_row, 1.0, 0.0)
    earlier = jnp.where(iota((agents, agents), 0) < iota((agents, agents), 1), 1.0, 0.0)
    ranks = matmul(key_mask.astype(jnp.bfloat16), earlier.astype(jnp.bfloat16))
    rank = jnp.sum(ranks * key_mask, axis=0, keepdims=True)
    slot = key_row * per_peer + rank.astype(jnp.int32)
    placing = jnp.where(iota((agents, agents), 0) == slot, 1.0, 0.0).astype(jnp.bfloat16)
    returns_row = jnp.broadcast_to(returns_ref[...], (8, agents)).astype(jnp.bfloat16)
    targets_row = times_trans(returns_row, placing)

    team_sums = team_total(flight, team_send, team_recv)
    sub = iota((8, agents), 0)
    tail = jnp.where(sub == 1, team_sums[TEAMS : TEAMS + 1, 0:1], targets_row)
    tail_send[...] = jnp.where(sub == 2, team_sums[TEAMS + 1 : TEAMS + 2, 0:1], tail)
    tail_recv[env] = tail_send[...]
    tail_flight = [
        remote(tail_send, tail_recv.at[env], tail_ss.at[d], tail_rs.at[d], peer)
        for d, peer in enumerate(env_peers)
    ]
    message = ((share(team_sums) - features.astype(jnp.float32)) * inv_peers).astype(jnp.bfloat16)
    hidden = jnp.tanh(own_part + matmul(message, wc_ref[...])).astype(jnp.bfloat16)
    outgoing = matmul(placing, hidden).reshape(env_devs, per_device, width)
    rows_send[...] = outgoing.astype(jnp.bfloat16)
    rows_recv[env] = rows_send[env]
    groups = ENV_DEV if per_peer % 16 == 0 else 1
    group_rows = per_device // groups

    def trade(group, source, target, send_one, recv_one):
        here = pl.ds(group * group_rows, group_rows)
        return [
            remote(
                source.at[peer[1], here],
                target.at[env, here],
                send_one.at[group, d],
                recv_one.at[group, d],
                peer,
            )
            for d, peer in enumerate(env_peers)
        ]

    rows_flight = [trade(g, rows_send, rows_recv, rows_ss, rows_rs) for g in range(groups)]

    logits = matmul(hidden, wp_ref[...])
    raised = jnp.exp(logits)
    totals = jnp.sum(raised, axis=-1, keepdims=True)
    probs_all = raised / totals
    log_probs = logits - jnp.log(totals)
    lane = iota((agents, actions_all), 1).astype(jnp.float32)
    chosen = jnp.where(lane == column(action_ref[...].astype(jnp.float32)), 1.0, 0.0)
    log_chosen = jnp.sum(chosen * log_probs, axis=-1, keepdims=True)
    ratios = jnp.exp(log_chosen - column(logp_ref[...]))
    for copy in tail_flight:
        copy.wait()
    adv_total = jnp.sum(tail_recv[:, 1, 0:1], axis=0, keepdims=True)
    adv_total_sq = jnp.sum(tail_recv[:, 2, 0:1], axis=0, keepdims=True)
    adv_mean = adv_total / agent_total
    adv_var = adv_total_sq / agent_total - adv_mean * adv_mean
    scaled = (column(adv_row) - adv_mean) / jnp.sqrt(adv_var + NORM_EPS)
    delta_grad = -ratios * scaled + KL_WEIGHT * (ratios - 1.0)
    logit_grad = (delta_grad * (chosen - probs_all)).astype(jnp.bfloat16)
    policy_back = times_trans(logit_grad, wp_ref[...])
    policy_part = trans_times(hidden, logit_grad)
    target_rows = tail_recv[:, 0, :].astype(jnp.bfloat16)

    kept_items = []
    back_flight = []
    for item in range(ENV_DEV):
        if item < groups:
            for copy in rows_flight[item]:
                copy.wait()
        here = slice(item * per_peer, (item + 1) * per_peer)
        rows_in = rows_recv[:, here, :].astype(jnp.float32).reshape(ENV_AGENTS, width)
        row_id = iota((ENV_AGENTS, env_devs), 0)
        pick = jnp.where(row_id // per_peer == iota((ENV_AGENTS, env_devs), 1), 1.0, 0.0)
        spread = matmul(pick.astype(jnp.bfloat16), target_rows)
        wanted = iota((ENV_AGENTS, agents), 0) % per_peer + item * per_peer + env * per_device
        keep = iota((ENV_AGENTS, agents), 1) == wanted
        targets = jnp.sum(jnp.where(keep, spread, 0.0), axis=1, keepdims=True)
        back, *kept = critic_item(
            rows_in, targets, gain_ref[...], wq_ref[...], wk_ref[...], wv_ref[...]
        )
        back = back.astype(jnp.float32).reshape(env_devs, per_peer, width)
        back_send[:, here, :] = back.astype(jnp.bfloat16)
        kept_items.append(kept)
        if groups > 1 or item == ENV_DEV - 1:
            group = item if groups > 1 else 0
            back_flight += trade(group, back_send, back_recv, back_ss, back_rs)
    back_recv[env] = back_send[env]

    def place(bit):
        if bit < team_bits:
            step = 1 << (team_bits - 1 - bit)
            mine = (team // step) % 2
            return mine, (team + (1 - 2 * mine) * step, env)
        step = 1 << (stages - 1 - bit)
        mine = (env // step) % 2
        return mine, (team, env + (1 - 2 * mine) * step)

    places = [place(bit) for bit in range(stages)]

    def start(i, stage):
        bit = orders[i][stage]
        axis = sum(1 for b in range(bit) if b not in orders[i][:stage])
        mine, peer = places[bit]
        before = (slice(None),) * axis
        if stage == 0:
            source = ins[i].at[before + (1 - mine,)]
        else:
            source = send[i][stage - 1]
            source[...] = sums[i][stage - 1][before + (1 - mine,)].astype(jnp.bfloat16)
        copy = remote(source, recv[i][stage], send_sem.at[i, stage], recv_sem.at[i, stage], peer)
        return copy, before + (mine,)

    pending = [None] * count

    def advance(i, stage):
        copy, kept = pending[i]
        copy.wait()
        held = ins[i] if stage == 0 else sums[i][stage - 1]
        total = held[kept].astype(jnp.float32) + recv[i][stage][...].astype(jnp.float32)
        if stage == stages - 1:
            parts_ref[:, edges[i] : edges[i + 1]] = total
        else:
            sums[i][stage][...] = total
            pending[i] = start(i, stage + 1)

    def emit(i, values):
        if not scatter:
            at = edges[i]
            for value in values:
                parts_ref[:, at : at + value.shape[1]] = value.astype(jnp.bfloat16)
                at += value.shape[1]
            return
        at = 0
        for value in values:
            cut = value.reshape(ins[i].shape[:-1] + (value.shape[1],)).astype(jnp.bfloat16)
            ins[i][..., at : at + value.shape[1]] = cut
            at += value.shape[1]
        pending[i] = start(i, 0)

    critic_parts = []
    for which in (1, 2):
        total = trans_times(kept_items[0][0], kept_items[0][which])
        for kept in kept_items[1:]:
            total = total + trans_times(kept[0], kept[which])
        critic_parts.append(total)
    emit(3, critic_parts)
    emit(2, [policy_part])

    for copy in back_flight:
        copy.wait()
    critic_grad = trans_times(placing, back_recv[...].reshape(agents, width))
    hidden_full = hidden.astype(jnp.float32)
    pre_grad = (policy_back + critic_grad) * (1.0 - hidden_full * hidden_full)
    pre_grad = pre_grad.astype(jnp.bfloat16)
    message_grad = times_trans(pre_grad, wc_ref[...])
    msg_send[...] = jnp.dot(
        team_low.astype(jnp.float32),
        message_grad,
        precision=lax.Precision.HIGHEST,
        preferred_element_type=jnp.float32,
    )
    flight = team_exchange(msg_send, msg_recv, msg_ss, msg_rs)
    emit(0, [trans_times(features, pre_grad)])
    emit(1, [trans_times(message, pre_grad)])
    if scatter:
        advance(3, 0)
        advance(2, 0)
    base = times_trans(pre_grad, wh_ref[...])
    message_sums = team_total(flight, msg_send, msg_recv)
    out_ref[...] = (base + (share(message_sums) - message_grad) * inv_peers).astype(jnp.bfloat16)
    if scatter:
        for stage in range(1, stages):
            for i in (0, 1):
                advance(i, stage - 1)
            for i in (3, 2):
                advance(i, stage)
        for i in (0, 1):
            advance(i, stages - 1)


def body(
    features,
    team_of,
    env_of,
    actions,
    old_logp,
    advantages,
    returns,
    w_hidden,
    w_comm,
    w_policy,
    norm_gain,
    w_query,
    w_key,
    w_value,
):
    agents, width = features.shape
    team_devs, env_devs = lax.axis_size("team"), lax.axis_size("env")
    devices = team_devs * env_devs
    team_bits, env_bits = log2(team_devs), log2(env_devs)
    stages = team_bits + env_bits
    full = jnp.float32
    rows = width // devices
    scatter = width % devices == 0 and rows % 16 == 0
    widths = [width, width, w_policy.shape[1], 2 * width]
    team_order = list(range(team_bits))[::-1]
    env_order = list(range(team_bits, stages))[::-1]
    first = team_order + env_order
    second = team_order[:1] + env_order + team_order[1:]
    orders = [first, first, second, second]
    per_device = ENV_DEV * ENV_AGENTS // env_devs
    low = jnp.bfloat16
    dma = pltpu.SemaphoreType.DMA

    def both(shape, dtype, copies):
        return [pltpu.VMEM(shape, dtype), pltpu.VMEM((copies,) + shape, dtype)]

    trade = (env_devs, per_device, width)
    agent_inputs = [team_of, env_of, actions, old_logp, advantages, returns.astype(full)]
    agent_inputs = [value[None, :] for value in agent_inputs]
    agent_inputs += [features, w_hidden, w_comm, w_policy, norm_gain[None, :]]
    agent_inputs += [w_query, w_key, w_value[None, :]]
    scratch = [pltpu.VMEM(value.shape, value.dtype) for value in agent_inputs]
    scratch += [dma((len(agent_inputs),))]
    scratch += both((8, width), full, team_devs - 1) * 2
    scratch += [pltpu.VMEM(trade, low)] * 2
    scratch += both((8, agents), full, env_devs)
    scratch += [pltpu.VMEM(trade, low)] * 2
    scratch += [dma((team_devs - 1,))] * 4 + [dma((ENV_DEV, env_devs - 1))] * 2
    scratch += [dma((env_devs - 1,))] * 2 + [dma((ENV_DEV, env_devs - 1))] * 2
    if scatter:

        def left(columns_in, stage, dtype):
            return pltpu.VMEM((2,) * (stages - 1 - stage) + (rows, columns_in), dtype)

        scratch += [left(c, -1, low) for c in widths]
        scratch += [left(c, s, low) for c in widths for s in range(stages)]
        scratch += [left(c, s, full) for c in widths for s in range(stages - 1)]
        scratch += [left(c, s + 1, low) for c in widths for s in range(stages - 1)]
        scratch += [dma((len(widths), stages))] * 2
        out_parts = jax.ShapeDtypeStruct((rows, sum(widths)), full)
    else:
        out_parts = jax.ShapeDtypeStruct((width, sum(widths)), low)
    grad_input, parts = pl.pallas_call(
        functools.partial(window_kernel, team_devs, env_devs, orders, scatter),
        out_shape=(jax.ShapeDtypeStruct((agents, width), low), out_parts),
        in_specs=[pl.BlockSpec(memory_space=pltpu.HBM)] * 14,
        out_specs=(pl.BlockSpec(memory_space=pltpu.VMEM),) * 2,
        scratch_shapes=scratch,
        compiler_params=pltpu.CompilerParams(
            collective_id=0, has_side_effects=True, vmem_limit_bytes=56 * 1024 * 1024
        ),
        cost_estimate=pl.CostEstimate(
            flops=11_000_000_000, bytes_accessed=6_000_000, transcendentals=1_000_000
        ),
    )(*agent_inputs)
    if not scatter:
        parts = lax.psum_scatter(
            parts.astype(full), ("team", "env"), scatter_dimension=0, tiled=True
        )
    edges = [0]
    for wide in (width, width, w_policy.shape[1], width, width):
        edges.append(edges[-1] + wide)
    return (grad_input, *[parts[:, a:b] for a, b in zip(edges[:-1], edges[1:])])


def solution(mesh):
    in_specs = (
        P(("team", "env"), None),
        P(("team", "env")),
        P(("team", "env")),
        P(("team", "env")),
        P(("team", "env")),
        P(("team", "env")),
        P(("team", "env")),
        P(),
        P(),
        P(),
        P(),
        P(),
        P(),
        P(),
    )
    out_specs = (
        P(("team", "env"), None),
        P(("team", "env"), None),
        P(("team", "env"), None),
        P(("team", "env"), None),
        P(("team", "env"), None),
        P(("team", "env"), None),
    )
    return jax.shard_map(body, mesh=mesh, in_specs=in_specs, out_specs=out_specs, check_vma=False)
```
